32 devices in a mesh: nodes: 32 (over z, y, x, core).
Axes of the slice: x: 2, y: 2, z: 4, core: 2. Of those that a mesh axis runs over, the one named last changes fastest.
Arguments:
- features: bfloat16 [262144, 256], P('nodes'), may hold values from -6 to 6
- cluster_ids: int32 [262144], P('nodes'), may hold values from 0 to 16383, as said below
- tile_cols: int32 [128, 6], P('nodes'), may hold values from 0 to 127, as said below
- tile_counts: int32 [128], P('nodes'), may hold values from 1 to 6
- adjacency: bfloat16 [128, 6, 128, 128], P('nodes'), may hold values from -0.5 to 0.5
- w_first: bfloat16 [256, 256], replicated, may hold values from -0.375 to 0.375
- w_second: bfloat16 [256, 256], replicated, may hold values from -0.375 to 0.375
Outputs:
- unpooled: bfloat16 [262144, 256], P('nodes')
The draws below stay inside these ranges and needn't reach their ends.
Inputs may be any that keep to these rules, and one draw needn't show every extreme that they name: `cluster_ids`: cluster c is held by device c // 512. Exactly 256 fine nodes of each device name clusters of other devices; at most 16 of them name clusters of any one other device, among at most 4 distinct clusters of it. `tile_cols`: tile s holds clusters s * 128 to s * 128 + 127; the column tiles named for a tile row of device p are tiles of devices p - 1, p and p + 1.
All inputs are finite; a program needn't handle non-finite values.
Results may differ from the reference program's by a relative error of at most 0.0051.
Values may be sent and summed in bfloat16 or wider, within the bound.
A program may use at most 64 MiB of HBM per device.

```python
import jax
import jax.numpy as jnp
from jax import lax

F = 256
FINE_DEV = 8192
CL_DEV = 512
TILE = 128
KT = 6
CAP = 16
DCAP = 4
BND = 256
NFINE = 262144
NCLUS = 16384
TILES_DEV = 4
NTILES = 128
N_NODES = 32


def draw_cluster_ids(key, part):
    key_star, key_devices = jax.random.split(jax.random.fold_in(key, 11))
    target = jax.random.randint(key_star, (), 0, N_NODES)
    device_keys = jax.random.split(key_devices, N_NODES)
    devices = jnp.arange(N_NODES, dtype=jnp.int32)

    def one_device(dev_key, device):
        key_a, key_b, key_c, key_d, key_e = jax.random.split(dev_key, 5)
        filled = jnp.where(device == target, (target + 1) % N_NODES, target)
        positions = (N_NODES - 1) * CAP
        spots = jnp.arange(positions, dtype=jnp.int32)
        owner_of = (device + 1 + spots // CAP) % N_NODES
        slot_of = spots % CAP
        ranking = jax.random.permutation(key_a, positions).astype(jnp.int32)
        scores = jnp.where(owner_of == filled, ranking - positions, ranking)
        picked = jnp.argsort(scores, stable=True)[:BND]
        picked_owner = owner_of[picked]
        picked_slot = slot_of[picked]
        bases = jax.random.randint(key_b, (N_NODES,), 0, CL_DEV)
        extra = jax.random.randint(key_c, (BND,), 0, DCAP)
        member = jnp.where(picked_slot < DCAP, picked_slot, extra)
        within = (bases[picked_owner] + member * (CL_DEV // DCAP)) % CL_DEV
        boundary_ids = picked_owner * CL_DEV + within
        interior = device * CL_DEV + jax.random.randint(key_d, (FINE_DEV,), 0, CL_DEV)
        places = jax.random.permutation(key_e, FINE_DEV)[:BND]
        return interior.at[places].set(boundary_ids)
    result = jax.vmap(one_device)(device_keys, devices)
    return result.reshape(-1).astype(jnp.int32)


def draw_tile_cols(key, part):
    sub_key = jax.random.fold_in(key, 21)
    tile_ids = jnp.arange(NTILES, dtype=jnp.int32)
    holder = tile_ids // TILES_DEV
    lowest = jnp.maximum(holder - 1, 0) * TILES_DEV
    highest = jnp.minimum(holder + 2, N_NODES) * TILES_DEV
    raw_ints = jax.random.randint(sub_key, (NTILES, KT), 0, 1 << 20)
    columns = lowest[:, None] + raw_ints % (highest - lowest)[:, None]
    columns = columns.at[:, 0].set(tile_ids)
    return columns.astype(jnp.int32)


def draw_tile_counts(key, part):
    key_a, key_b = jax.random.split(jax.random.fold_in(key, 31))
    counts = jax.random.randint(key_a, (NTILES,), 1, KT + 1)
    fullest = jax.random.randint(key_b, (), 0, NTILES)
    counts = counts.at[fullest].set(KT)
    return counts.astype(jnp.int32)


def steps_of(rng, shape, cuts, least, high):
    def one(axis_at, blocks):
        heights = jax.random.uniform(jax.random.fold_in(jax.random.fold_in(rng, 6), axis_at), (blocks,), jnp.float32, least / len(cuts), high / len(cuts))
        return jnp.repeat(jnp.exp(heights), shape[axis_at] // blocks).reshape((-1,) + (1,) * (len(shape) - axis_at - 1))

    loudness = one(*cuts[0])
    for cut in cuts[1:]:
        loudness = loudness * one(*cut)
    return loudness


def scatter_about(stream_key, shape, spread, reach, cuts=(), kind=jnp.bfloat16):
    values = jax.random.normal(stream_key, shape, jnp.float32) * spread
    if len(cuts) > 0:
        values = steps_of(stream_key, shape, cuts, -0.22, 0.18) * values
    return jnp.clip(values, min=-reach, max=reach).astype(kind)


def setup_inputs(seed: int = 0) -> dict:
    key_list = jax.random.split(jax.random.key(seed), 8)
    return {
        "features": scatter_about(key_list[0], (NFINE, F), 1.0, 6.0, ((0, 32),)),
        "cluster_ids": draw_cluster_ids(jax.random.fold_in(key_list[7], 71), 0),
        "tile_cols": draw_tile_cols(jax.random.fold_in(key_list[7], 71), 0),
        "tile_counts": draw_tile_counts(jax.random.fold_in(key_list[7], 71), 0),
        "adjacency": scatter_about(key_list[4], (NTILES, KT, TILE, TILE), ((TILE * KT) ** -0.5), 0.5, ((0, 32),)),
        "w_first": scatter_about(key_list[5], (F, F), F ** -0.5, 0.375),
        "w_second": scatter_about(key_list[6], (F, F), F ** -0.5, 0.375),
    }


def convolve(values, tile_cols, tile_counts, adjacency):
    tiles = values.reshape(NTILES, TILE, F)
    live = (jnp.arange(KT, dtype=jnp.int32)[None, :] < tile_counts[:, None]).astype(jnp.float32)

    def one_tile(pieces):
        weights, cols, keep = pieces
        picked = tiles[cols].astype(jnp.float32)
        scaled = weights.astype(jnp.float32) * keep[:, None, None]
        return jnp.einsum('kij,kjf->if', scaled, picked)
    result = lax.map(one_tile, (adjacency, tile_cols, live))
    return result.reshape(NCLUS, F)

def reference(features, cluster_ids, tile_cols, tile_counts, adjacency, w_first, w_second):
    feature_blocks = features.reshape(N_NODES, FINE_DEV, F)
    id_blocks = cluster_ids.reshape(N_NODES, FINE_DEV)

    def add_block(running, pieces):
        sums_acc, counts_acc = running
        rows_x, ids_x = pieces
        sums_acc = sums_acc.at[ids_x].add(rows_x.astype(jnp.float32))
        counts_acc = counts_acc.at[ids_x].add(jnp.ones((FINE_DEV,), jnp.float32))
        return ((sums_acc, counts_acc), None)
    start = (jnp.zeros((NCLUS, F), jnp.float32), jnp.zeros((NCLUS,), jnp.float32))
    (sums_all, counts_all), _ = lax.scan(add_block, start, (feature_blocks, id_blocks))
    pooled = (sums_all / jnp.sqrt(counts_all + 1.0)[:, None]).astype(jnp.bfloat16)
    first_proj = jnp.dot(pooled, w_first, preferred_element_type=jnp.float32).astype(jnp.bfloat16)
    hidden = jnp.maximum(convolve(first_proj, tile_cols, tile_counts, adjacency), 0.0).astype(jnp.bfloat16)
    second_proj = jnp.dot(hidden, w_second, preferred_element_type=jnp.float32).astype(jnp.bfloat16)
    coarse = convolve(second_proj, tile_cols, tile_counts, adjacency).astype(jnp.bfloat16)

    def unpool_block(pieces):
        rows_x, ids_x = pieces
        return (rows_x.astype(jnp.float32) + coarse[ids_x].astype(jnp.float32)).astype(jnp.bfloat16)
    result = lax.map(unpool_block, (feature_blocks, id_blocks))
    return result.reshape(NFINE, F)
```

```python
import functools

import jax
import jax.numpy as jnp
from jax import lax
from jax.experimental import pallas as pl
from jax.experimental.pallas import tpu as pltpu
from jax.sharding import PartitionSpec as P

CL_DEV = 512
DCAP = 4
LANES = 128
MSG = 16
ROWS = 8
F32 = jnp.float32
BF16 = jnp.bfloat16
I32 = jnp.int32
MESH = pl.DeviceIdType.MESH
CONTRACT_LANES = (((1,), (1,)), ((), ()))
CONTRACT_ROWS = (((0,), (0,)), ((), ()))


def dot(a, b, dims=None):
    if dims is None:
        return jnp.dot(a, b, preferred_element_type=F32)
    return lax.dot_general(a, b, dims, preferred_element_type=F32)


def iota(shape, axis):
    return lax.broadcasted_iota(I32, shape, axis)


def ones_where(mask):
    return jnp.where(mask, jnp.float32(1), jnp.float32(0)).astype(BF16)


def hot_of_rows(keys, ids):
    return jnp.concatenate(
        [ones_where(keys == ids[r : r + 1, :]) for r in range(ids.shape[0])], axis=1
    )


def place(rows, slots, part, group):
    row = iota((rows, slots), 0)
    slot = iota((rows, slots), 1)
    at = (slot // DCAP) * group + part * DCAP + slot % DCAP
    return ones_where(row == at)


def take(rows, slots, part, group):
    slot = iota((slots, rows), 0)
    row = iota((slots, rows), 1)
    at = (slot // DCAP) * group + part * DCAP + slot % DCAP
    return ones_where(row == at)


def find_slots(counts, me):
    high = counts.shape[0]
    per = CL_DEV // LANES
    slots = high // per * DCAP
    row = iota((high, LANES), 0)
    present = jnp.logical_and(counts > 0.5, row // per != me)
    hot = ones_where(present)
    before = ones_where(iota((LANES, LANES), 0) < iota((LANES, LANES), 1))
    ones = jnp.ones((LANES, LANES), BF16)
    row_total = dot(hot, ones).astype(BF16)
    r0, r1 = iota((high, high), 0), iota((high, high), 1)
    earlier = ones_where(jnp.logical_and(r0 // per == r1 // per, r1 < r0))
    rank = dot(hot, before) + dot(earlier, row_total)
    lows = iota((LANES, LANES), 0).astype(F32).astype(BF16)
    s0, h1 = iota((slots, high), 0), iota((slots, high), 1)
    low = jnp.zeros((slots, LANES), F32)
    top = jnp.zeros((slots, LANES), F32)
    number = jnp.zeros((slots, LANES), F32)
    for r in range(DCAP):
        mine = jnp.logical_and(present, jnp.abs(rank - r) < 0.5)
        chosen = ones_where(mine)
        weighed = jnp.where(mine, counts, 0.0).astype(BF16)
        pick = jnp.logical_and(s0 % DCAP == r, s0 // DCAP == h1 // per)
        pick_one = ones_where(pick)
        pick_top = jnp.where(pick, h1 % per, 0).astype(F32).astype(BF16)
        flag = dot(chosen, ones).astype(BF16)
        low = low + dot(pick_one, dot(chosen, lows).astype(BF16))
        number = number + dot(pick_one, dot(weighed, ones).astype(BF16))
        top = top + dot(pick_top, flag)
    return low, top, number


def coarse_kernel(
    n, ids_ref, cols_ref, live_ref, feat_ref, adj_ref, w1_ref, w2_ref,
    table_ref, key_ref,
    fbuf, fsem, cnt_ref, acc_ref, sacc_ref, skey_ref, msg, rec, msg2, rec2, win1, win2,
    send1, recv1, send2, recv2, hsend, hrecv,
):
    me = lax.axis_index("nodes")
    fine, width = fbuf.shape
    chunk = ROWS * LANES
    chunks = fine // chunk
    tiles, kt = cols_ref.shape
    tile = adj_ref.shape[2]
    slots = n * DCAP
    per = CL_DEV // LANES
    high = n * per
    half = width // 2

    def load(c):
        at = pl.ds(c * chunk, chunk)
        return pltpu.make_async_copy(feat_ref.at[at], fbuf.at[at], fsem.at[c])

    for c in range(chunks):
        load(c).start()

    barrier = pltpu.get_barrier_semaphore()

    def greet(j, x):
        pl.semaphore_signal(barrier, inc=1, device_id=(lax.rem(me + j, n),), device_id_type=MESH)
        return x

    lax.fori_loop(1, n, greet, 0)

    cnt_ref[...] = jnp.zeros_like(cnt_ref)

    def count(c, x):
        ids = ids_ref[pl.ds(pl.multiple_of(c * ROWS, ROWS), ROWS), :]
        hi = hot_of_rows(iota((high, LANES), 0), ids // LANES)
        lo = hot_of_rows(iota((LANES, LANES), 0), ids % LANES)
        cnt_ref[...] += dot(hi, lo, CONTRACT_LANES)
        return x

    lax.fori_loop(0, chunks, count, 0)

    low, top, number = find_slots(cnt_ref[...], me)
    owner = iota((slots, LANES), 0) // DCAP
    key = (owner * CL_DEV).astype(F32) + top * LANES + low
    key = jnp.where(number > 0.5, key, -1.0).astype(I32)
    skey_ref[...] = key
    key_ref[...] = key.T[0:ROWS, :]

    for c in range(chunks):
        load(c).wait()

    sacc_ref[...] = jnp.zeros_like(sacc_ref)

    def pool_slots(c, x):
        ids = ids_ref[pl.ds(pl.multiple_of(c * ROWS, ROWS), ROWS), :]
        rows = fbuf[pl.ds(pl.multiple_of(c * chunk, chunk), chunk), :]
        sacc_ref[...] += dot(hot_of_rows(skey_ref[...], ids), rows)
        return x

    lax.fori_loop(0, chunks, pool_slots, 0)

    sums = sacc_ref[...].astype(BF16)
    parts = [sums[:, :half], sums[:, half:], low.astype(BF16), (number * 4.0 + top).astype(BF16)]
    packed = jnp.zeros((MSG * n, LANES), F32)
    for i, part in enumerate(parts):
        packed = packed + dot(place(MSG * n, slots, i, MSG), part)
    msg[...] = packed.astype(BF16)
    mine = pl.ds(pl.multiple_of(me * MSG, MSG), MSG)
    rec[mine, :] = jnp.zeros((MSG, LANES), BF16)
    rec2[mine, :] = jnp.zeros((MSG, LANES), BF16)
    pl.semaphore_wait(barrier, n - 1)

    def send(src, dst, ssem, rsem, peer):
        return pltpu.make_async_remote_copy(
            src_ref=src.at[pl.ds(pl.multiple_of(peer * MSG, MSG), MSG)],
            dst_ref=dst.at[mine],
            send_sem=ssem.at[peer],
            recv_sem=rsem.at[me],
            device_id=(peer,),
            device_id_type=MESH,
        )

    def arrived(src, dst, ssem, rsem, peer):
        at = pl.ds(pl.multiple_of(peer * MSG, MSG), MSG)
        return pltpu.make_async_remote_copy(
            src_ref=src.at[at],
            dst_ref=dst.at[at],
            send_sem=ssem.at[peer],
            recv_sem=rsem.at[peer],
            device_id=(peer,),
            device_id_type=MESH,
        )

    def exchange_start(*refs):
        def go(j, x):
            send(*refs, lax.rem(me + j, n)).start()
            return x

        lax.fori_loop(1, n, go, 0)

    def exchange_wait(*refs):
        def go(j, x):
            arrived(*refs, lax.rem(me + j, n)).wait_recv()
            return x

        lax.fori_loop(1, n, go, 0)

    def exchange_end(*refs):
        def go(j, x):
            arrived(*refs, lax.rem(me + j, n)).wait_send()
            return x

        lax.fori_loop(1, n, go, 0)

    first = (msg, rec, send1, recv1)
    second = (msg2, rec2, send2, recv2)
    exchange_start(*first)

    acc_ref[...] = jnp.zeros_like(acc_ref)

    def pool_own(c, x):
        ids = ids_ref[pl.ds(pl.multiple_of(c * ROWS, ROWS), ROWS), :] - me * CL_DEV
        rows = fbuf[pl.ds(pl.multiple_of(c * chunk, chunk), chunk), :]
        acc_ref[...] += dot(hot_of_rows(iota((CL_DEV, LANES), 0), ids), rows)
        return x

    lax.fori_loop(0, chunks, pool_own, 0)

    eye = iota((LANES, LANES), 0) == iota((LANES, LANES), 1)
    own_counts = jnp.concatenate(
        [
            jnp.sum(jnp.where(eye, cnt_ref[pl.ds(me * per + a, 1), :], 0.0), axis=1, keepdims=True)
            for a in range(per)
        ],
        axis=0,
    )

    exchange_wait(*first)
    got = rec[...]
    got_left, got_right, got_low, got_code = (
        dot(take(MSG * n, slots, i, MSG), got) for i in range(4)
    )
    got_code = got_code.astype(I32)
    got_number = got_code // 4
    got_id = (got_code % 4) * LANES + got_low.astype(I32)
    got_id = jnp.where(got_number > 0, got_id, -1)
    answer_hot = jnp.concatenate(
        [ones_where(got_id == iota((slots, LANES), 1) + a * LANES) for a in range(per)], axis=1
    )
    got_all = jnp.concatenate(
        [got_left.astype(BF16), got_right.astype(BF16), got_number.astype(F32).astype(BF16)], axis=1
    )
    more = dot(answer_hot, got_all, CONTRACT_ROWS)
    counts = own_counts + more[:, width : width + 1]
    pooled = ((acc_ref[...] + more[:, :width]) / jnp.sqrt(counts + 1.0)).astype(BF16)

    def halo(win, i):
        up = pltpu.make_async_remote_copy(
            src_ref=win.at[pl.ds(tiles, tiles)],
            dst_ref=win.at[pl.ds(0, tiles)],
            send_sem=hsend.at[i],
            recv_sem=hrecv.at[i],
            device_id=(lax.rem(me + 1, n),),
            device_id_type=MESH,
        )
        down = pltpu.make_async_remote_copy(
            src_ref=win.at[pl.ds(tiles, tiles)],
            dst_ref=win.at[pl.ds(2 * tiles, tiles)],
            send_sem=hsend.at[i + 1],
            recv_sem=hrecv.at[i + 1],
            device_id=(lax.rem(me + n - 1, n),),
            device_id_type=MESH,
        )
        return up, down

    def fill_halo(win, values, i):
        win[pl.ds(tiles, tiles), :, :] = values.reshape(tiles, tile, width)
        up, down = halo(win, i)
        low_end, high_end = me == 0, me == n - 1

        @pl.when(jnp.logical_not(high_end))
        def _():
            up.start()

        @pl.when(jnp.logical_not(low_end))
        def _():
            down.start()

        @pl.when(low_end)
        def _():
            win[pl.ds(0, tiles), :, :] = jnp.zeros((tiles, tile, width), BF16)

        @pl.when(high_end)
        def _():
            win[pl.ds(2 * tiles, tiles), :, :] = jnp.zeros((tiles, tile, width), BF16)

        @pl.when(jnp.logical_not(low_end))
        def _():
            up.wait_recv()
            down.wait_send()

        @pl.when(jnp.logical_not(high_end))
        def _():
            down.wait_recv()
            up.wait_send()

    def convolve(win):
        result = []
        for t in range(tiles):
            total = jnp.zeros((tile, width), F32)
            for k in range(kt):
                at = jnp.clip(cols_ref[t, k] - (me - 1) * tiles, 0, 3 * tiles - 1)
                keep = jnp.broadcast_to(k < live_ref[0, t], (tile, tile))
                weights = jnp.where(keep, adj_ref[t, k].astype(F32), 0.0).astype(BF16)
                total = total + dot(weights, win[at])
            result.append(total)
        return jnp.concatenate(result, axis=0)

    fill_halo(win1, dot(pooled, w1_ref[...]).astype(BF16), 0)
    hidden = jnp.maximum(convolve(win1), 0.0).astype(BF16)
    fill_halo(win2, dot(hidden, w2_ref[...]).astype(BF16), 2)
    coarse = convolve(win2).astype(BF16)
    answers = dot(answer_hot, coarse).astype(BF16)
    packed = dot(place(MSG * n, slots, 0, MSG), answers[:, :half])
    packed = packed + dot(place(MSG * n, slots, 1, MSG), answers[:, half:])
    msg2[...] = packed.astype(BF16)
    exchange_start(*second)
    table_ref[pl.ds(0, CL_DEV), :] = coarse
    exchange_end(*first)
    exchange_wait(*second)
    back = rec2[...]
    table_ref[pl.ds(CL_DEV, slots), :] = jnp.concatenate(
        [dot(take(MSG * n, slots, i, MSG), back) for i in range(2)], axis=1
    ).astype(BF16)
    exchange_end(*second)


def unpool_kernel(ids_ref, key_ref, table_ref, feat_ref, out_ref):
    me = lax.axis_index("nodes")
    own = me * CL_DEV
    own_keys = [iota((1, LANES), 1) + (own + a * LANES) for a in range(CL_DEV // LANES)]
    slots = key_ref.shape[1]
    table = table_ref[...]
    slot_keys = [key_ref[0:1, a * LANES : (a + 1) * LANES] for a in range(slots // LANES)]
    for r in range(ROWS):
        at = pl.ds(r * LANES, LANES)
        ids = jnp.broadcast_to(ids_ref[r : r + 1, :], (LANES, LANES)).T
        hot = jnp.concatenate([ones_where(ids == key) for key in own_keys + slot_keys], axis=1)
        value = feat_ref[at, :].astype(F32) + dot(hot, table)
        out_ref[at, :] = value.astype(BF16)


def local(features, cluster_ids, tile_cols, tile_counts, adjacency, w_first, w_second):
    n = lax.axis_size("nodes")
    fine, width = features.shape
    tiles, _ = tile_cols.shape
    tile = adjacency.shape[2]
    slots = n * DCAP
    high = n * (CL_DEV // LANES)
    chunk = ROWS * LANES
    chunks = fine // chunk
    ids = cluster_ids.reshape(fine // LANES, LANES)
    vmem = pl.BlockSpec(memory_space=pltpu.VMEM)
    smem = pl.BlockSpec(memory_space=pltpu.SMEM)
    hbm = pl.BlockSpec(memory_space=pl.ANY)
    dma = pltpu.SemaphoreType.DMA
    table, keys = pl.pallas_call(
        functools.partial(coarse_kernel, n),
        out_shape=(
            jax.ShapeDtypeStruct((CL_DEV + slots, width), BF16),
            jax.ShapeDtypeStruct((ROWS, slots), I32),
        ),
        in_specs=[vmem, smem, smem, hbm, vmem, vmem, vmem],
        out_specs=(vmem, vmem),
        scratch_shapes=[
            pltpu.VMEM((fine, width), BF16),
            dma((chunks,)),
            pltpu.VMEM((high, LANES), F32),
            pltpu.VMEM((CL_DEV, width), F32),
            pltpu.VMEM((slots, width), F32),
            pltpu.VMEM((slots, LANES), I32),
            pltpu.VMEM((MSG * n, LANES), BF16),
            pltpu.VMEM((MSG * n, LANES), BF16),
            pltpu.VMEM((MSG * n, LANES), BF16),
            pltpu.VMEM((MSG * n, LANES), BF16),
            pltpu.VMEM((3 * tiles, tile, width), BF16),
            pltpu.VMEM((3 * tiles, tile, width), BF16),
            dma((n,)),
            dma((n,)),
            dma((n,)),
            dma((n,)),
            dma((4,)),
            dma((4,)),
        ],
        compiler_params=pltpu.CompilerParams(
            collective_id=0, has_side_effects=True, vmem_limit_bytes=48 * 1024 * 1024
        ),
    )(ids, tile_cols, tile_counts.reshape(1, tiles), features, adjacency, w_first, w_second)
    return pl.pallas_call(
        unpool_kernel,
        grid=(chunks,),
        out_shape=jax.ShapeDtypeStruct((fine, width), BF16),
        in_specs=[
            pl.BlockSpec((ROWS, LANES), lambda i: (i, 0)),
            pl.BlockSpec((ROWS, slots), lambda i: (0, 0)),
            pl.BlockSpec((CL_DEV + slots, width), lambda i: (0, 0)),
            pl.BlockSpec((chunk, width), lambda i: (i, 0)),
        ],
        out_specs=pl.BlockSpec((chunk, width), lambda i: (i, 0)),
        compiler_params=pltpu.CompilerParams(vmem_limit_bytes=32 * 1024 * 1024),
    )(ids, keys, table, features)


def solution(mesh):
    placed = (
        P("nodes", None),
        P("nodes"),
        P("nodes", None),
        P("nodes"),
        P("nodes", None, None, None),
        P(),
        P(),
    )
    return jax.shard_map(
        local, mesh=mesh, in_specs=placed, out_specs=P("nodes", None), check_vma=False
    )
```

```python
import functools

import jax
import jax.numpy as jnp
from jax import lax
from jax.experimental import pallas as pl
from jax.experimental.pallas import tpu as pltpu
from jax.sharding import PartitionSpec as P

CL_DEV = 512
DCAP = 4
LANES = 128
MSG = 16
VMEM_BYTES = 63 * 1024 * 1024
PACK = 16
DSHIFT = 2
LSHIFT = 7
PSHIFT = 2
ROWS = 8
F32 = jnp.float32
BF16 = jnp.bfloat16
I32 = jnp.int32
I16 = jnp.int16
MESH = pl.DeviceIdType.MESH
CONTRACT_LANES = (((1,), (1,)), ((), ()))
CONTRACT_ROWS = (((0,), (0,)), ((), ()))


def dot(a, b, dims=None):
    if dims is None:
        return jnp.dot(a, b, preferred_element_type=F32)
    return lax.dot_general(a, b, dims, preferred_element_type=F32)


def iota(shape, axis):
    return lax.broadcasted_iota(I32, shape, axis)


def ones_where(mask):
    return jnp.where(mask, jnp.float32(1), jnp.float32(0)).astype(BF16)


def hot16(a, b):
    return jnp.where(a == b, jnp.ones((), BF16), jnp.zeros((), BF16))


def short_rows(row, count):
    one = jnp.broadcast_to(row, (PACK, LANES)).astype(I16)
    return jnp.concatenate([one] * (count // PACK), axis=0)


def hot_of_rows(keys, ids):
    return jnp.concatenate(
        [hot16(keys, short_rows(ids[r : r + 1, :], keys.shape[0])) for r in range(ids.shape[0])],
        axis=1,
    )


def place(rows, slots, part, group):
    row = iota((rows, slots), 0)
    slot = iota((rows, slots), 1)
    at = (slot >> DSHIFT) * group + part * DCAP + (slot & (DCAP - 1))
    return ones_where(row == at)


def take(rows, slots, part, group):
    slot = iota((slots, rows), 0)
    row = iota((slots, rows), 1)
    at = (slot >> DSHIFT) * group + part * DCAP + (slot & (DCAP - 1))
    return ones_where(row == at)


def find_slots(counts, me):
    high = counts.shape[0]
    per = CL_DEV // LANES
    slots = high // per * DCAP
    row = iota((high, LANES), 0)
    present = jnp.logical_and(counts > 0.5, (row >> PSHIFT) != me)
    hot = ones_where(present)
    before = ones_where(iota((LANES, LANES), 0) < iota((LANES, LANES), 1))
    ones = jnp.ones((LANES, LANES), BF16)
    row_total = dot(hot, ones).astype(BF16)
    r0, r1 = iota((high, high), 0), iota((high, high), 1)
    earlier = ones_where(jnp.logical_and((r0 >> PSHIFT) == (r1 >> PSHIFT), r1 < r0))
    rank = dot(hot, before) + dot(earlier, row_total)
    lows = iota((LANES, LANES), 0).astype(F32).astype(BF16)
    s0, h1 = iota((slots, high), 0), iota((slots, high), 1)
    low = jnp.zeros((slots, LANES), F32)
    top = jnp.zeros((slots, LANES), F32)
    number = jnp.zeros((slots, LANES), F32)
    for r in range(DCAP):
        mine = jnp.logical_and(present, jnp.abs(rank - r) < 0.5)
        chosen = ones_where(mine)
        weighed = jnp.where(mine, counts, 0.0).astype(BF16)
        pick = jnp.logical_and((s0 & (DCAP - 1)) == r, (s0 >> DSHIFT) == (h1 >> PSHIFT))
        pick_one = ones_where(pick)
        pick_top = jnp.where(pick, h1 & (per - 1), 0).astype(F32).astype(BF16)
        flag = dot(chosen, ones).astype(BF16)
        low = low + dot(pick_one, dot(chosen, lows).astype(BF16))
        number = number + dot(pick_one, dot(weighed, ones).astype(BF16))
        top = top + dot(pick_top, flag)
    return low, top, number


def coarse_kernel(
    n, ids_hbm, cols_hbm, live_hbm, feat_ref, adj_hbm, w1_hbm, w2_hbm,
    table_ref, key_ref,
    ids_ref, cols_ref, live_ref, adj_ref, w1_ref, w2_ref, isem, fbuf, fsem, cnt_ref, acc_ref, sacc_ref, skey_ref, msg, rec, msg2, rec2, win1, win2,
    send1, recv1, send2, recv2, hsend, hrecv,
):
    me = lax.axis_index("nodes")
    fine, width = fbuf.shape
    chunk = ROWS * LANES
    chunks = fine // chunk
    tiles, kt = cols_ref.shape
    tile = adj_ref.shape[2]
    slots = n * DCAP
    per = CL_DEV // LANES
    high = n * per
    half = width // 2

    def load(c):
        at = pl.ds(c * chunk, chunk)
        return pltpu.make_async_copy(feat_ref.at[at], fbuf.at[at], fsem.at[c])

    pairs = (
        (ids_hbm, ids_ref), (cols_hbm, cols_ref), (live_hbm, live_ref),
        (adj_hbm, adj_ref), (w1_hbm, w1_ref), (w2_hbm, w2_ref),
    )
    loads = [pltpu.make_async_copy(a, b, isem.at[i]) for i, (a, b) in enumerate(pairs)]
    loads[0].start()
    for c in range(chunks):
        load(c).start()
    for copy in loads[1:]:
        copy.start()

    barrier = pltpu.get_barrier_semaphore()

    def greet(j, x):
        pl.semaphore_signal(barrier, inc=1, device_id=(lax.rem(me + j, n),), device_id_type=MESH)
        return x

    lax.fori_loop(1, n, greet, 0)

    cnt_ref[...] = jnp.zeros_like(cnt_ref)

    def count(c, x):
        ids = ids_ref[pl.ds(pl.multiple_of(c * ROWS, ROWS), ROWS), :]
        hi = hot_of_rows(iota((high, LANES), 0).astype(I16), ids >> LSHIFT)
        lo = hot_of_rows(iota((LANES, LANES), 0).astype(I16), ids & (LANES - 1))
        cnt_ref[...] += dot(hi, lo, CONTRACT_LANES)
        return x

    loads[0].wait()
    lax.fori_loop(0, chunks, count, 0)

    low, top, number = find_slots(cnt_ref[...], me)
    owner = iota((slots, LANES), 0) >> DSHIFT
    key = (owner * CL_DEV).astype(F32) + top * LANES + low
    key = jnp.where(number > 0.5, key, -1.0).astype(I32)
    skey_ref[...] = key.astype(I16)
    key_ref[...] = key.T[0:ROWS, :]

    for c in range(chunks):
        load(c).wait()

    sacc_ref[...] = jnp.zeros_like(sacc_ref)

    def pool_slots(c, x):
        ids = ids_ref[pl.ds(pl.multiple_of(c * ROWS, ROWS), ROWS), :]
        rows = fbuf[pl.ds(pl.multiple_of(c * chunk, chunk), chunk), :]
        sacc_ref[...] += dot(hot_of_rows(skey_ref[...], ids), rows)
        return x

    lax.fori_loop(0, chunks, pool_slots, 0)

    sums = sacc_ref[...].astype(BF16)
    parts = [sums[:, :half], sums[:, half:], low.astype(BF16), (number * 4.0 + top).astype(BF16)]
    packed = jnp.zeros((MSG * n, LANES), F32)
    for i, part in enumerate(parts):
        packed = packed + dot(place(MSG * n, slots, i, MSG), part)
    msg[...] = packed.astype(BF16)
    mine = pl.ds(pl.multiple_of(me * MSG, MSG), MSG)
    rec[mine, :] = jnp.zeros((MSG, LANES), BF16)
    rec2[mine, :] = jnp.zeros((MSG, LANES), BF16)
    pl.semaphore_wait(barrier, n - 1)

    def send(src, dst, ssem, rsem, peer):
        return pltpu.make_async_remote_copy(
            src_ref=src.at[pl.ds(pl.multiple_of(peer * MSG, MSG), MSG)],
            dst_ref=dst.at[mine],
            send_sem=ssem.at[peer],
            recv_sem=rsem.at[me],
            device_id=(peer,),
            device_id_type=MESH,
        )

    def arrived(src, dst, ssem, rsem, peer):
        at = pl.ds(pl.multiple_of(peer * MSG, MSG), MSG)
        return pltpu.make_async_remote_copy(
            src_ref=src.at[at],
            dst_ref=dst.at[at],
            send_sem=ssem.at[peer],
            recv_sem=rsem.at[peer],
            device_id=(peer,),
            device_id_type=MESH,
        )

    def exchange_start(*refs):
        def go(j, x):
            send(*refs, lax.rem(me + j, n)).start()
            return x

        lax.fori_loop(1, n, go, 0)

    def exchange_wait(*refs):
        def go(j, x):
            arrived(*refs, lax.rem(me + j, n)).wait_recv()
            return x

        lax.fori_loop(1, n, go, 0)

    def exchange_end(*refs):
        def go(j, x):
            arrived(*refs, lax.rem(me + j, n)).wait_send()
            return x

        lax.fori_loop(1, n, go, 0)

    first = (msg, rec, send1, recv1)
    second = (msg2, rec2, send2, recv2)
    exchange_start(*first)

    acc_ref[...] = jnp.zeros_like(acc_ref)

    def pool_own(c, x):
        ids = ids_ref[pl.ds(pl.multiple_of(c * ROWS, ROWS), ROWS), :] - me * CL_DEV
        rows = fbuf[pl.ds(pl.multiple_of(c * chunk, chunk), chunk), :]
        acc_ref[...] += dot(hot_of_rows(iota((CL_DEV, LANES), 0).astype(I16), ids), rows)
        return x

    lax.fori_loop(0, chunks, pool_own, 0)

    for copy in loads[1:]:
        copy.wait()
    eye = iota((LANES, LANES), 0) == iota((LANES, LANES), 1)
    own_counts = jnp.concatenate(
        [
            jnp.sum(jnp.where(eye, cnt_ref[pl.ds(me * per + a, 1), :], 0.0), axis=1, keepdims=True)
            for a in range(per)
        ],
        axis=0,
    )

    exchange_wait(*first)
    got = rec[...]
    got_left, got_right, got_low, got_code = (
        dot(take(MSG * n, slots, i, MSG), got) for i in range(4)
    )
    got_code = got_code.astype(I32)
    got_number = got_code >> 2
    got_id = (got_code & 3) * LANES + got_low.astype(I32)
    got_id = jnp.where(got_number > 0, got_id, -1)
    answer_hot = jnp.concatenate(
        [ones_where(got_id == iota((slots, LANES), 1) + a * LANES) for a in range(per)], axis=1
    )
    got_all = jnp.concatenate(
        [got_left.astype(BF16), got_right.astype(BF16), got_number.astype(F32).astype(BF16)], axis=1
    )
    more = dot(answer_hot, got_all, CONTRACT_ROWS)
    counts = own_counts + more[:, width : width + 1]
    pooled = ((acc_ref[...] + more[:, :width]) * lax.rsqrt(counts + 1.0)).astype(BF16)

    def halo(win, i):
        up = pltpu.make_async_remote_copy(
            src_ref=win.at[pl.ds(tiles, tiles)],
            dst_ref=win.at[pl.ds(0, tiles)],
            send_sem=hsend.at[i],
            recv_sem=hrecv.at[i],
            device_id=(lax.rem(me + 1, n),),
            device_id_type=MESH,
        )
        down = pltpu.make_async_remote_copy(
            src_ref=win.at[pl.ds(tiles, tiles)],
            dst_ref=win.at[pl.ds(2 * tiles, tiles)],
            send_sem=hsend.at[i + 1],
            recv_sem=hrecv.at[i + 1],
            device_id=(lax.rem(me + n - 1, n),),
            device_id_type=MESH,
        )
        return up, down

    def fill_halo(win, values, i):
        win[pl.ds(tiles, tiles), :, :] = values.reshape(tiles, tile, width)
        up, down = halo(win, i)
        low_end, high_end = me == 0, me == n - 1

        @pl.when(jnp.logical_not(high_end))
        def _():
            up.start()

        @pl.when(jnp.logical_not(low_end))
        def _():
            down.start()

        @pl.when(low_end)
        def _():
            win[pl.ds(0, tiles), :, :] = jnp.zeros((tiles, tile, width), BF16)

        @pl.when(high_end)
        def _():
            win[pl.ds(2 * tiles, tiles), :, :] = jnp.zeros((tiles, tile, width), BF16)

        @pl.when(jnp.logical_not(low_end))
        def _():
            up.wait_recv()
            down.wait_send()

        @pl.when(jnp.logical_not(high_end))
        def _():
            down.wait_recv()
            up.wait_send()

    def convolve(win):
        result = []
        for t in range(tiles):
            total = jnp.zeros((tile, width), F32)
            for k in range(kt):
                at = jnp.clip(cols_ref[t, k] - (me - 1) * tiles, 0, 3 * tiles - 1)
                keep = jnp.broadcast_to(k < live_ref[0, t], (tile, tile))
                weights = jnp.where(keep, adj_ref[t, k].astype(F32), 0.0).astype(BF16)
                total = total + dot(weights, win[at])
            result.append(total)
        return jnp.concatenate(result, axis=0)

    fill_halo(win1, dot(pooled, w1_ref[...]).astype(BF16), 0)
    hidden = jnp.maximum(convolve(win1), 0.0).astype(BF16)
    fill_halo(win2, dot(hidden, w2_ref[...]).astype(BF16), 2)
    coarse = convolve(win2).astype(BF16)
    answers = dot(answer_hot, coarse).astype(BF16)
    packed = dot(place(MSG * n, slots, 0, MSG), answers[:, :half])
    packed = packed + dot(place(MSG * n, slots, 1, MSG), answers[:, half:])
    msg2[...] = packed.astype(BF16)
    exchange_start(*second)
    table_ref[pl.ds(0, CL_DEV), :] = coarse
    exchange_end(*first)
    exchange_wait(*second)
    back = rec2[...]
    table_ref[pl.ds(CL_DEV, slots), :] = jnp.concatenate(
        [dot(take(MSG * n, slots, i, MSG), back) for i in range(2)], axis=1
    ).astype(BF16)
    exchange_end(*second)


def unpool_kernel(ids_ref, key_ref, table_ref, feat_ref, out_ref):
    me = lax.axis_index("nodes")
    own = me * CL_DEV
    own_keys = [iota((1, LANES), 1) + (own + a * LANES) for a in range(CL_DEV // LANES)]
    slots = key_ref.shape[1]
    table = table_ref[...]
    slot_keys = [key_ref[0:1, a * LANES : (a + 1) * LANES] for a in range(slots // LANES)]
    keys = [short_rows(key, LANES) for key in own_keys + slot_keys]
    for r in range(ROWS):
        at = pl.ds(r * LANES, LANES)
        ids = jnp.broadcast_to(ids_ref[r : r + 1, :], (LANES, LANES)).T
        ids = ids.astype(I16)
        hot = jnp.concatenate([hot16(ids, key) for key in keys], axis=1)
        value = feat_ref[at, :].astype(F32) + dot(hot, table)
        out_ref[at, :] = value.astype(BF16)


def local(features, cluster_ids, tile_cols, tile_counts, adjacency, w_first, w_second):
    n = lax.axis_size("nodes")
    fine, width = features.shape
    tiles, _ = tile_cols.shape
    tile = adjacency.shape[2]
    slots = n * DCAP
    high = n * (CL_DEV // LANES)
    chunk = ROWS * LANES
    chunks = fine // chunk
    ids = cluster_ids.reshape(fine // LANES, LANES)
    vmem = pl.BlockSpec(memory_space=pltpu.VMEM)
    hbm = pl.BlockSpec(memory_space=pltpu.HBM)
    dma = pltpu.SemaphoreType.DMA
    table, keys = pl.pallas_call(
        functools.partial(coarse_kernel, n),
        out_shape=(
            jax.ShapeDtypeStruct((CL_DEV + slots, width), BF16),
            jax.ShapeDtypeStruct((ROWS, slots), I32),
        ),
        in_specs=[hbm] * 7,
        out_specs=(vmem, vmem),
        scratch_shapes=[
            pltpu.VMEM(ids.shape, I32),
            pltpu.SMEM(tile_cols.shape, I32),
            pltpu.SMEM((1, tiles), I32),
            pltpu.VMEM(adjacency.shape, BF16),
            pltpu.VMEM(w_first.shape, BF16),
            pltpu.VMEM(w_second.shape, BF16),
            dma((6,)),
            pltpu.VMEM((fine, width), BF16),
            dma((chunks,)),
            pltpu.VMEM((high, LANES), F32),
            pltpu.VMEM((CL_DEV, width), F32),
            pltpu.VMEM((slots, width), F32),
            pltpu.VMEM((slots, LANES), I16),
            pltpu.VMEM((MSG * n, LANES), BF16),
            pltpu.VMEM((MSG * n, LANES), BF16),
            pltpu.VMEM((MSG * n, LANES), BF16),
            pltpu.VMEM((MSG * n, LANES), BF16),
            pltpu.VMEM((3 * tiles, tile, width), BF16),
            pltpu.VMEM((3 * tiles, tile, width), BF16),
            dma((n,)),
            dma((n,)),
            dma((n,)),
            dma((n,)),
            dma((4,)),
            dma((4,)),
        ],
        compiler_params=pltpu.CompilerParams(
            collective_id=0, has_side_effects=True, vmem_limit_bytes=VMEM_BYTES
        ),
    )(ids, tile_cols, tile_counts.reshape(1, tiles), features, adjacency, w_first, w_second)
    return pl.pallas_call(
        unpool_kernel,
        grid=(chunks,),
        out_shape=jax.ShapeDtypeStruct((fine, width), BF16),
        in_specs=[
            pl.BlockSpec((ROWS, LANES), lambda i: (i, 0)),
            pl.BlockSpec((ROWS, slots), lambda i: (0, 0)),
            pl.BlockSpec((CL_DEV + slots, width), lambda i: (0, 0)),
            pl.BlockSpec((chunk, width), lambda i: (i, 0)),
        ],
        out_specs=pl.BlockSpec((chunk, width), lambda i: (i, 0)),
        compiler_params=pltpu.CompilerParams(vmem_limit_bytes=VMEM_BYTES),
    )(ids, keys, table, features)


def solution(mesh):
    placed = (
        P("nodes", None),
        P("nodes"),
        P("nodes", None),
        P("nodes"),
        P("nodes", None, None, None),
        P(),
        P(),
    )
    return jax.shard_map(
        local, mesh=mesh, in_specs=placed, out_specs=P("nodes", None), check_vma=False
    )
```

```python
import functools

import jax
import jax.numpy as jnp
from jax import lax
from jax.experimental import pallas as pl
from jax.experimental.pallas import tpu as pltpu
from jax.sharding import PartitionSpec as P

CL_DEV = 512
DCAP = 4
LANES = 128
MSG = 16
WIDE = 2
VMEM_BYTES = 63 * 1024 * 1024
PACK = 16
DSHIFT = 2
LSHIFT = 7
PSHIFT = 2
ROWS = 8
F32 = jnp.float32
BF16 = jnp.bfloat16
I32 = jnp.int32
I16 = jnp.int16
MESH = pl.DeviceIdType.MESH
CONTRACT_LANES = (((1,), (1,)), ((), ()))
CONTRACT_ROWS = (((0,), (0,)), ((), ()))


def dot(a, b, dims=None):
    if dims is None:
        return jnp.dot(a, b, preferred_element_type=F32)
    return lax.dot_general(a, b, dims, preferred_element_type=F32)


def iota(shape, axis):
    return lax.broadcasted_iota(I32, shape, axis)


def ones_where(mask):
    return jnp.where(mask, jnp.float32(1), jnp.float32(0)).astype(BF16)


def hot16(a, b):
    return jnp.where(a == b, jnp.ones((), BF16), jnp.zeros((), BF16))


def short_rows(row, count):
    one = jnp.broadcast_to(row, (PACK, LANES)).astype(I16)
    return jnp.concatenate([one] * (count // PACK), axis=0)


def hot_of_rows(keys, ids):
    return jnp.concatenate(
        [hot16(keys, short_rows(ids[r : r + 1, :], keys.shape[0])) for r in range(ids.shape[0])],
        axis=1,
    )


def place(rows, slots, part, group):
    row = iota((rows, slots), 0)
    slot = iota((rows, slots), 1)
    at = (slot >> DSHIFT) * group + part * DCAP + (slot & (DCAP - 1))
    return ones_where(row == at)


def take(rows, slots, part, group):
    slot = iota((slots, rows), 0)
    row = iota((slots, rows), 1)
    at = (slot >> DSHIFT) * group + part * DCAP + (slot & (DCAP - 1))
    return ones_where(row == at)


def find_slots(counts, me):
    high = counts.shape[0]
    per = CL_DEV // LANES
    slots = high // per * DCAP
    row = iota((high, LANES), 0)
    present = jnp.logical_and(counts > 0.5, (row >> PSHIFT) != me)
    hot = ones_where(present)
    before = ones_where(iota((LANES, LANES), 0) < iota((LANES, LANES), 1))
    ones = jnp.ones((LANES, LANES), BF16)
    row_total = dot(hot, ones).astype(BF16)
    r0, r1 = iota((high, high), 0), iota((high, high), 1)
    earlier = ones_where(jnp.logical_and((r0 >> PSHIFT) == (r1 >> PSHIFT), r1 < r0))
    rank = dot(hot, before) + dot(earlier, row_total)
    lows = iota((LANES, LANES), 0).astype(F32).astype(BF16)
    s0, h1 = iota((slots, high), 0), iota((slots, high), 1)
    low = jnp.zeros((slots, LANES), F32)
    top = jnp.zeros((slots, LANES), F32)
    number = jnp.zeros((slots, LANES), F32)
    for r in range(DCAP):
        mine = jnp.logical_and(present, jnp.abs(rank - r) < 0.5)
        chosen = ones_where(mine)
        weighed = jnp.where(mine, counts, 0.0).astype(BF16)
        pick = jnp.logical_and((s0 & (DCAP - 1)) == r, (s0 >> DSHIFT) == (h1 >> PSHIFT))
        pick_one = ones_where(pick)
        pick_top = jnp.where(pick, h1 & (per - 1), 0).astype(F32).astype(BF16)
        flag = dot(chosen, ones).astype(BF16)
        low = low + dot(pick_one, dot(chosen, lows).astype(BF16))
        number = number + dot(pick_one, dot(weighed, ones).astype(BF16))
        top = top + dot(pick_top, flag)
    return low, top, number


def coarse_kernel(
    n, ids_hbm, cols_hbm, live_hbm, feat_ref, adj_hbm, w1_hbm, w2_hbm,
    table_ref, key_ref,
    ids_ref, cols_ref, live_ref, adj_ref, w1_ref, w2_ref, isem, fbuf, fsem, cnt_ref, acc_ref, sacc_ref, skey_ref, msg, rec, msg2, rec2, win1, win2,
    send1, recv1, send2, recv2, hsend, hrecv,
):
    me = lax.axis_index("nodes")
    fine, width = fbuf.shape
    chunk = ROWS * LANES
    chunks = fine // chunk
    tiles, kt = cols_ref.shape
    tile = adj_ref.shape[2]
    slots = n * DCAP
    per = CL_DEV // LANES
    high = n * per
    half = width // 2

    def load(c):
        at = pl.ds(c * chunk, chunk)
        return pltpu.make_async_copy(feat_ref.at[at], fbuf.at[at], fsem.at[c])

    pairs = (
        (ids_hbm, ids_ref), (cols_hbm, cols_ref), (live_hbm, live_ref),
        (adj_hbm, adj_ref), (w1_hbm, w1_ref), (w2_hbm, w2_ref),
    )
    loads = [pltpu.make_async_copy(a, b, isem.at[i]) for i, (a, b) in enumerate(pairs)]
    loads[0].start()
    for c in range(chunks):
        load(c).start()
    for copy in loads[1:]:
        copy.start()

    barrier = pltpu.get_barrier_semaphore()

    def greet(j, x):
        pl.semaphore_signal(barrier, inc=1, device_id=(lax.rem(me + j, n),), device_id_type=MESH)
        return x

    lax.fori_loop(1, n, greet, 0)

    cnt_ref[...] = jnp.zeros_like(cnt_ref)

    def count(c, x):
        ids = ids_ref[pl.ds(pl.multiple_of(c * ROWS, ROWS), ROWS), :]
        hi = hot_of_rows(iota((high, LANES), 0).astype(I16), ids >> LSHIFT)
        lo = hot_of_rows(iota((LANES, LANES), 0).astype(I16), ids & (LANES - 1))
        cnt_ref[...] += dot(hi, lo, CONTRACT_LANES)
        return x

    loads[0].wait()
    lax.fori_loop(0, chunks, count, 0)

    low, top, number = find_slots(cnt_ref[...], me)
    owner = iota((slots, LANES), 0) >> DSHIFT
    key = (owner * CL_DEV).astype(F32) + top * LANES + low
    key = jnp.where(number > 0.5, key, -1.0).astype(I32)
    skey_ref[...] = key.astype(I16)
    key_ref[...] = key.T[0:ROWS, :]

    for c in range(chunks):
        load(c).wait()

    sacc_ref[...] = jnp.zeros_like(sacc_ref)

    def pool_slots(c, x):
        ids = ids_ref[pl.ds(pl.multiple_of(c * ROWS, ROWS), ROWS), :]
        rows = fbuf[pl.ds(pl.multiple_of(c * chunk, chunk), chunk), :]
        sacc_ref[...] += dot(hot_of_rows(skey_ref[...], ids), rows)
        return x

    lax.fori_loop(0, chunks, pool_slots, 0)

    sums = sacc_ref[...].astype(BF16)
    parts = [sums[:, :half], sums[:, half:], low.astype(BF16), (number * 4.0 + top).astype(BF16)]
    packed = jnp.zeros((MSG * n, LANES), F32)
    for i, part in enumerate(parts):
        packed = packed + dot(place(MSG * n, slots, i, MSG), part)
    msg[...] = packed.astype(BF16)
    mine = pl.ds(pl.multiple_of(me * MSG, MSG), MSG)
    rec[mine, :] = jnp.zeros((MSG, LANES), BF16)
    rec2[mine, :] = jnp.zeros((MSG, LANES), BF16)
    pl.semaphore_wait(barrier, n - 1)

    def send(src, dst, ssem, rsem, peer):
        return pltpu.make_async_remote_copy(
            src_ref=src.at[pl.ds(pl.multiple_of(peer * MSG, MSG), MSG)],
            dst_ref=dst.at[mine],
            send_sem=ssem.at[peer],
            recv_sem=rsem.at[me],
            device_id=(peer,),
            device_id_type=MESH,
        )

    def arrived(src, dst, ssem, rsem, peer):
        at = pl.ds(pl.multiple_of(peer * MSG, MSG), MSG)
        return pltpu.make_async_remote_copy(
            src_ref=src.at[at],
            dst_ref=dst.at[at],
            send_sem=ssem.at[peer],
            recv_sem=rsem.at[peer],
            device_id=(peer,),
            device_id_type=MESH,
        )

    def exchange_start(*refs):
        def go(j, x):
            send(*refs, lax.rem(me + j, n)).start()
            return x

        lax.fori_loop(1, n, go, 0)

    def exchange_wait(*refs):
        def go(j, x):
            arrived(*refs, lax.rem(me + j, n)).wait_recv()
            return x

        lax.fori_loop(1, n, go, 0)

    def exchange_end(*refs):
        def go(j, x):
            arrived(*refs, lax.rem(me + j, n)).wait_send()
            return x

        lax.fori_loop(1, n, go, 0)

    first = (msg, rec, send1, recv1)
    second = (msg2, rec2, send2, recv2)
    exchange_start(*first)

    acc_ref[...] = jnp.zeros_like(acc_ref)

    def pool_own(c, x):
        ids = ids_ref[pl.ds(pl.multiple_of(c * ROWS, ROWS), ROWS), :] - me * CL_DEV
        rows = fbuf[pl.ds(pl.multiple_of(c * chunk, chunk), chunk), :]
        acc_ref[...] += dot(hot_of_rows(iota((CL_DEV, LANES), 0).astype(I16), ids), rows)
        return x

    lax.fori_loop(0, chunks, pool_own, 0)

    for copy in loads[1:]:
        copy.wait()
    eye = iota((LANES, LANES), 0) == iota((LANES, LANES), 1)
    own_counts = jnp.concatenate(
        [
            jnp.sum(jnp.where(eye, cnt_ref[pl.ds(me * per + a, 1), :], 0.0), axis=1, keepdims=True)
            for a in range(per)
        ],
        axis=0,
    )

    exchange_wait(*first)
    got = rec[...]
    got_left, got_right, got_low, got_code = (
        dot(take(MSG * n, slots, i, MSG), got) for i in range(4)
    )
    got_code = got_code.astype(I32)
    got_number = got_code >> 2
    got_id = (got_code & 3) * LANES + got_low.astype(I32)
    got_id = jnp.where(got_number > 0, got_id, -1)
    answer_hot = jnp.concatenate(
        [ones_where(got_id == iota((slots, LANES), 1) + a * LANES) for a in range(per)], axis=1
    )
    got_all = jnp.concatenate(
        [got_left.astype(BF16), got_right.astype(BF16), got_number.astype(F32).astype(BF16)], axis=1
    )
    more = dot(answer_hot, got_all, CONTRACT_ROWS)
    counts = own_counts + more[:, width : width + 1]
    pooled = ((acc_ref[...] + more[:, :width]) * lax.rsqrt(counts + 1.0)).astype(BF16)

    def halo(win, i):
        up = pltpu.make_async_remote_copy(
            src_ref=win.at[pl.ds(tiles, tiles)],
            dst_ref=win.at[pl.ds(0, tiles)],
            send_sem=hsend.at[i],
            recv_sem=hrecv.at[i],
            device_id=(lax.rem(me + 1, n),),
            device_id_type=MESH,
        )
        down = pltpu.make_async_remote_copy(
            src_ref=win.at[pl.ds(tiles, tiles)],
            dst_ref=win.at[pl.ds(2 * tiles, tiles)],
            send_sem=hsend.at[i + 1],
            recv_sem=hrecv.at[i + 1],
            device_id=(lax.rem(me + n - 1, n),),
            device_id_type=MESH,
        )
        return up, down

    def fill_halo(win, values, i):
        win[pl.ds(tiles, tiles), :, :] = values.reshape(tiles, tile, width)
        up, down = halo(win, i)
        low_end, high_end = me == 0, me == n - 1

        @pl.when(jnp.logical_not(high_end))
        def _():
            up.start()

        @pl.when(jnp.logical_not(low_end))
        def _():
            down.start()

        @pl.when(low_end)
        def _():
            win[pl.ds(0, tiles), :, :] = jnp.zeros((tiles, tile, width), BF16)

        @pl.when(high_end)
        def _():
            win[pl.ds(2 * tiles, tiles), :, :] = jnp.zeros((tiles, tile, width), BF16)

        @pl.when(jnp.logical_not(low_end))
        def _():
            up.wait_recv()
            down.wait_send()

        @pl.when(jnp.logical_not(high_end))
        def _():
            down.wait_recv()
            up.wait_send()

    def convolve(win):
        result = []
        for t in range(tiles):
            total = jnp.zeros((tile, width), F32)
            for k in range(kt):
                at = jnp.clip(cols_ref[t, k] - (me - 1) * tiles, 0, 3 * tiles - 1)
                keep = jnp.broadcast_to(k < live_ref[0, t], (tile, tile))
                weights = jnp.where(keep, adj_ref[t, k].astype(F32), 0.0).astype(BF16)
                total = total + dot(weights, win[at])
            result.append(total)
        return jnp.concatenate(result, axis=0)

    fill_halo(win1, dot(pooled, w1_ref[...]).astype(BF16), 0)
    hidden = jnp.maximum(convolve(win1), 0.0).astype(BF16)
    fill_halo(win2, dot(hidden, w2_ref[...]).astype(BF16), 2)
    coarse = convolve(win2).astype(BF16)
    answers = dot(answer_hot, coarse).astype(BF16)
    packed = dot(place(MSG * n, slots, 0, MSG), answers[:, :half])
    packed = packed + dot(place(MSG * n, slots, 1, MSG), answers[:, half:])
    msg2[...] = packed.astype(BF16)
    exchange_start(*second)
    table_ref[pl.ds(0, CL_DEV), :] = coarse
    exchange_end(*first)
    exchange_wait(*second)
    back = rec2[...]
    table_ref[pl.ds(CL_DEV, slots), :] = jnp.concatenate(
        [dot(take(MSG * n, slots, i, MSG), back) for i in range(2)], axis=1
    ).astype(BF16)
    exchange_end(*second)


def unpool_kernel(ids_ref, key_ref, table_ref, feat_ref, out_ref):
    me = lax.axis_index("nodes")
    own = me * CL_DEV
    own_keys = [iota((1, LANES), 1) + (own + a * LANES) for a in range(CL_DEV // LANES)]
    slots = key_ref.shape[1]
    table = table_ref[...]
    slot_keys = [key_ref[0:1, a * LANES : (a + 1) * LANES] for a in range(slots // LANES)]
    keys = [short_rows(key, LANES) for key in own_keys + slot_keys]
    for r in range(ids_ref.shape[0]):
        at = pl.ds(r * LANES, LANES)
        ids = jnp.broadcast_to(ids_ref[r : r + 1, :], (LANES, LANES)).T
        ids = ids.astype(I16)
        hot = jnp.concatenate([hot16(ids, key) for key in keys], axis=1)
        value = feat_ref[at, :].astype(F32) + dot(hot, table)
        out_ref[at, :] = value.astype(BF16)


def local(features, cluster_ids, tile_cols, tile_counts, adjacency, w_first, w_second):
    n = lax.axis_size("nodes")
    fine, width = features.shape
    tiles, _ = tile_cols.shape
    tile = adjacency.shape[2]
    slots = n * DCAP
    high = n * (CL_DEV // LANES)
    chunk = ROWS * LANES
    chunks = fine // chunk
    ids = cluster_ids.reshape(fine // LANES, LANES)
    vmem = pl.BlockSpec(memory_space=pltpu.VMEM)
    hbm = pl.BlockSpec(memory_space=pltpu.HBM)
    dma = pltpu.SemaphoreType.DMA
    table, keys = pl.pallas_call(
        functools.partial(coarse_kernel, n),
        out_shape=(
            jax.ShapeDtypeStruct((CL_DEV + slots, width), BF16),
            jax.ShapeDtypeStruct((ROWS, slots), I32),
        ),
        in_specs=[hbm] * 7,
        out_specs=(vmem, vmem),
        scratch_shapes=[
            pltpu.VMEM(ids.shape, I32),
            pltpu.SMEM(tile_cols.shape, I32),
            pltpu.SMEM((1, tiles), I32),
            pltpu.VMEM(adjacency.shape, BF16),
            pltpu.VMEM(w_first.shape, BF16),
            pltpu.VMEM(w_second.shape, BF16),
            dma((6,)),
            pltpu.VMEM((fine, width), BF16),
            dma((chunks,)),
            pltpu.VMEM((high, LANES), F32),
            pltpu.VMEM((CL_DEV, width), F32),
            pltpu.VMEM((slots, width), F32),
            pltpu.VMEM((slots, LANES), I16),
            pltpu.VMEM((MSG * n, LANES), BF16),
            pltpu.VMEM((MSG * n, LANES), BF16),
            pltpu.VMEM((MSG * n, LANES), BF16),
            pltpu.VMEM((MSG * n, LANES), BF16),
            pltpu.VMEM((3 * tiles, tile, width), BF16),
            pltpu.VMEM((3 * tiles, tile, width), BF16),
            dma((n,)),
            dma((n,)),
            dma((n,)),
            dma((n,)),
            dma((4,)),
            dma((4,)),
        ],
        compiler_params=pltpu.CompilerParams(
            collective_id=0, has_side_effects=True, vmem_limit_bytes=VMEM_BYTES
        ),
    )(ids, tile_cols, tile_counts.reshape(1, tiles), features, adjacency, w_first, w_second)
    return pl.pallas_call(
        unpool_kernel,
        grid=(chunks // WIDE,),
        out_shape=jax.ShapeDtypeStruct((fine, width), BF16),
        in_specs=[
            pl.BlockSpec((ROWS * WIDE, LANES), lambda i: (i, 0)),
            pl.BlockSpec((ROWS, slots), lambda i: (0, 0)),
            pl.BlockSpec((CL_DEV + slots, width), lambda i: (0, 0)),
            pl.BlockSpec((chunk * WIDE, width), lambda i: (i, 0)),
        ],
        out_specs=pl.BlockSpec((chunk * WIDE, width), lambda i: (i, 0)),
        compiler_params=pltpu.CompilerParams(vmem_limit_bytes=VMEM_BYTES),
    )(ids, keys, table, features)


def solution(mesh):
    placed = (
        P("nodes", None),
        P("nodes"),
        P("nodes", None),
        P("nodes"),
        P("nodes", None, None, None),
        P(),
        P(),
    )
    return jax.shard_map(
        local, mesh=mesh, in_specs=placed, out_specs=P("nodes", None), check_vma=False
    )
```
